512 devices in a mesh: dp: 16 (over y_hi, x, core), tensor: 32 (over z, y_lo).
Axes of the slice: x: 4, y: 4 (y_hi: 2, y_lo: 2; y = y_hi * 2 + y_lo), z: 16, core: 2. Of those that a mesh axis runs over, the one named last changes fastest.
Arguments:
- x_rotated: bfloat16 [1024, 10240], P('tensor', 'dp'), may hold values from -6 to 6
- block_scales: float32 [1024, 80], P('tensor', 'dp'), may hold values from 0.3 to 3
- grad_act: bfloat16 [1024, 36864], P('dp', 'tensor'), may hold values from -6 to 6
- w_in: bfloat16 [10240, 36864], P('dp', 'tensor'), may hold values from -0.0625 to 0.0625
Outputs:
- grad_input: bfloat16 [1024, 10240], P('tensor', 'dp')
- grad_weight: bfloat16 [10240, 36864], P('dp', 'tensor')
The draws below stay inside these ranges and needn't reach their ends.
All inputs are finite; a program needn't handle non-finite values.
Results may differ from the reference program's by a relative error of at most 0.034.
Values may be sent and summed in bfloat16 or wider, within the bound.
No kernel may reach another device: no remote copies, remote signals or barrier semaphores. Data moves between devices by JAX's collectives and lax.ppermute only.
A program may use at most 64 MiB of HBM per device.

```python
import math
import jax
import jax.numpy as jnp
from jax import lax

D = 10240
FF_DEV = 1152
D_DEV = 640
FF = 36864
TOKENS = 1024
N_DP = 16
N_TENSOR = 32


def shard_levels(rng, extent, cuts, low, top_value):
    def one(axis_at, blocks):
        heights = jax.random.uniform(jax.random.fold_in(jax.random.fold_in(rng, 6), axis_at), (blocks,), jnp.float32, low / len(cuts), top_value / len(cuts))
        return jnp.repeat(jnp.exp(heights), extent[axis_at] // blocks).reshape((-1,) + (1,) * (len(extent) - axis_at - 1))

    level = one(*cuts[0])
    for cut in cuts[1:]:
        level = level * one(*cut)
    return level


def centred(stream_key, dims, deviation, limit, split=(), kind=jnp.bfloat16):
    factor_of = shard_levels(stream_key, dims, split, -0.22, 0.18) if split else 1.0
    result = jax.random.normal(stream_key, dims, jnp.float32) * deviation * factor_of
    return jnp.minimum(jnp.maximum(result, -limit), limit).astype(kind)


def setup_inputs(seed: int = 0) -> dict:
    streams_of = jax.random.split(jax.random.key(seed), 5)
    x_rotated = centred(streams_of[0], (TOKENS, D), 1.0, 6.0, ((0, 32), (1, 16)))
    block_scales = jnp.clip(jnp.exp(math.log(3.0) - 2.3025851 * jax.random.uniform(streams_of[1], (TOKENS, D // 128), jnp.float32) ** shard_levels(streams_of[1], (TOKENS, D // 128), ((0, 32), (1, 16)), -0.2, 0.2)), 0.3, 3.0)
    grad_act = centred(streams_of[2], (TOKENS, FF), 1.0, 6.0, ((0, 16), (1, 32)))
    w_in = centred(streams_of[3], (D, FF), D ** -0.5, 0.0625, ((0, 16), (1, 32)))
    return dict(x_rotated=x_rotated, block_scales=block_scales, grad_act=grad_act, w_in=w_in)


def hadamard_table():
    index = lax.iota(jnp.int32, 128)
    common = jnp.bitwise_and(index[:, None], index[None, :])
    parity = jnp.zeros((128, 128), jnp.int32)
    for shift in range(7):
        parity = parity + jnp.bitwise_and(jnp.right_shift(common, shift), 1)
    signs = 1.0 - 2.0 * (parity % 2).astype(jnp.float32)
    return signs / math.sqrt(128.0)

def decode(coded, scales):
    count = coded.shape[0]
    blocks = coded.astype(jnp.float32).reshape(count, scales.shape[1], 128) * scales[:, :, None]
    turned = jnp.einsum('rbk,kj->rbj', blocks, hadamard_table(), precision=lax.Precision.HIGHEST)
    return turned.reshape(count, coded.shape[1]).astype(jnp.bfloat16)

def gelu_slope(value):
    cdf = 0.5 * (1.0 + jax.scipy.special.erf(value / math.sqrt(2.0)))
    pdf = jnp.exp(-0.5 * value * value) / math.sqrt(2.0 * math.pi)
    return cdf + value * pdf

def reference(x_rotated, block_scales, grad_act, w_in):
    inputs = decode(x_rotated, block_scales)
    input_slabs = jnp.transpose(inputs.reshape(TOKENS, N_DP, D_DEV), (1, 0, 2))
    weight_slabs = w_in.reshape(N_DP, D_DEV, FF)

    def one_slab(acc, pair):
        part = jnp.dot(pair[0], pair[1], preferred_element_type=jnp.float32)
        return (acc + part.astype(jnp.bfloat16).astype(jnp.float32), None)
    pre, _ = lax.scan(one_slab, jnp.zeros((TOKENS, FF), jnp.float32), (input_slabs, weight_slabs))
    grad_pre = (grad_act.astype(jnp.float32) * gelu_slope(pre)).astype(jnp.bfloat16)

    def one_block(acc, block):
        start = (block * FF_DEV).astype(jnp.int32)
        cols_pre = lax.dynamic_slice_in_dim(grad_pre, start, FF_DEV, 1)
        cols_w = lax.dynamic_slice_in_dim(w_in, start, FF_DEV, 1)
        part = lax.dot_general(cols_pre, cols_w, (((1,), (1,)), ((), ())), preferred_element_type=jnp.float32)
        return (acc + part.astype(jnp.bfloat16).astype(jnp.float32), None)
    summed, _ = lax.scan(one_block, jnp.zeros((TOKENS, D), jnp.float32), jnp.arange(N_TENSOR, dtype=jnp.int32))
    total = lax.dot_general(inputs, grad_pre, (((0,), (0,)), ((), ())), preferred_element_type=jnp.float32)
    return (summed.astype(jnp.bfloat16), total.astype(jnp.bfloat16))
```

```python
import math

import jax
import jax.numpy as jnp
from jax import lax
from jax.sharding import Mesh
from jax.sharding import PartitionSpec as P

AXES = ("yh", "x", "c", "zq", "zc", "yl")
SIZES = (2, 4, 2, 8, 2, 2)
DP = ("yh", "x", "c")
TENSOR = ("zq", "zc", "yl")
SWAP = [(0, 1), (1, 0)]


def hadamard_table():
    index = lax.iota(jnp.int32, 128)
    common = jnp.bitwise_and(index[:, None], index[None, :])
    parity = jnp.zeros((128, 128), jnp.int32)
    for shift in range(7):
        parity = parity + jnp.bitwise_and(jnp.right_shift(common, shift), 1)
    signs = 1.0 - 2.0 * (parity % 2).astype(jnp.float32)
    return signs / math.sqrt(128.0)


def decode(coded, scales):
    count = coded.shape[0]
    blocks = coded.astype(jnp.float32).reshape(count, scales.shape[1], 128) * scales[:, :, None]
    turned = jnp.einsum("rbk,kj->rbj", blocks, hadamard_table(), precision=lax.Precision.HIGHEST)
    return turned.reshape(count, coded.shape[1]).astype(jnp.bfloat16)


def gelu_slope(value):
    cdf = 0.5 * (1.0 + jax.scipy.special.erf(value / math.sqrt(2.0)))
    pdf = jnp.exp(-0.5 * value * value) / math.sqrt(2.0 * math.pi)
    return cdf + value * pdf


def slope_grad(pre, grads):
    return (grads.astype(jnp.float32) * gelu_slope(pre)).astype(jnp.bfloat16)


def dot(a, b, dims):
    return lax.dot_general(a, b, (dims, ((), ())), preferred_element_type=jnp.float32)


def half(array, which):
    return lax.dynamic_index_in_dim(array, which, 0, keepdims=False)


def chunk_gradient(rows, grads, w_in, core):
    far = dot(half(rows, 1 - core), w_in, ((1,), (0,))).astype(jnp.bfloat16)
    far = lax.ppermute(far, "c", SWAP)
    near = dot(half(rows, core), w_in, ((1,), (0,)))
    near = (near + far.astype(jnp.float32)).astype(jnp.bfloat16)
    parts = lax.all_to_all(near, ("yh", "x"), 0, 0, tiled=True)
    pre = jnp.sum(parts.reshape(8, 32, -1).astype(jnp.float32), axis=0)
    grad = slope_grad(pre, grads)
    copies = jnp.broadcast_to(grad[None], (8,) + grad.shape).reshape(256, -1)
    mine = lax.all_to_all(copies, ("yh", "x"), 0, 0, tiled=True)
    other = lax.ppermute(mine, "c", SWAP)
    return mine, other


def in_core_order(mine, other, core):
    return jnp.where(core == 0, jnp.stack([mine, other]), jnp.stack([other, mine]))


def shards(x_rotated, block_scales, grad_act, w_in):
    core = lax.axis_index("c")
    side = lax.axis_index("yl")
    own = decode(x_rotated, block_scales)
    partner = lax.ppermute(own, "yl", SWAP)
    first = lax.all_gather(partner, ("zc", "zq"), axis=0, tiled=True)
    second = lax.ppermute(first, "yl", SWAP)
    grads = grad_act.reshape(2, 32, -1)
    sums, weights = [], []
    for rows, which in ((first, 1 - side), (second, side)):
        rows = rows.reshape(2, 256, -1)
        mine, other = chunk_gradient(rows, half(grads, which), w_in, core)
        grad_pre = in_core_order(mine, other, core).reshape(512, -1)
        weights.append(dot(rows.reshape(512, -1), grad_pre, ((0,), (0,))))
        part = dot(grad_pre, w_in, ((1,), (1,)))
        if not sums:
            sums.append(lax.ppermute(part.astype(jnp.bfloat16), "yl", SWAP))
        else:
            sums.append(part)
    part = (sums[1] + sums[0].astype(jnp.float32)).astype(jnp.bfloat16)
    blocks = lax.all_to_all(part, ("zc", "zq"), 0, 0, tiled=True)
    grad_input = jnp.sum(blocks.reshape(16, 32, -1).astype(jnp.float32), axis=0)
    grad_weight = (weights[0] + weights[1]).astype(jnp.bfloat16)
    return grad_input.astype(jnp.bfloat16), grad_weight


def solution(mesh):
    fine = Mesh(mesh.devices.reshape(SIZES), AXES)
    in_specs = (P(TENSOR, DP), P(TENSOR, DP), P(DP, TENSOR), P(DP, TENSOR))
    out_specs = (P(TENSOR, DP), P(DP, TENSOR))
    return jax.shard_map(shards, mesh=fine, in_specs=in_specs, out_specs=out_specs, check_vma=False)
```

```python
import math

import jax
import jax.numpy as jnp
from jax import lax
from jax.experimental import pallas as pl
from jax.experimental.pallas import tpu as pltpu
from jax.sharding import Mesh
from jax.sharding import PartitionSpec as P

AXES = ("yh", "x", "c", "z", "yl")
SIZES = (2, 4, 2, 16, 2)
DP = ("yh", "x", "c")
TENSOR = ("z", "yl")
SWAP = [(0, 1), (1, 0)]
PIECES = ((-4, 0, 4, 8), (-5, -1, 3, 7), (-3, 1, 5, 9), (-6, -2), (2, 6))
VMEM = pl.BlockSpec(memory_space=pltpu.VMEM)
SMEM = pl.BlockSpec(memory_space=pltpu.SMEM)
PARAMS = pltpu.CompilerParams(vmem_limit_bytes=24 * 1024 * 1024)


def hadamard_table():
    index = lax.iota(jnp.int32, 128)
    common = jnp.bitwise_and(index[:, None], index[None, :])
    parity = jnp.zeros((128, 128), jnp.int32)
    for shift in range(7):
        parity = parity + jnp.bitwise_and(jnp.right_shift(common, shift), 1)
    signs = 1.0 - 2.0 * (parity % 2).astype(jnp.float32)
    return signs / math.sqrt(128.0)


def decode(coded, scales):
    count = coded.shape[0]
    blocks = coded.astype(jnp.float32).reshape(count, scales.shape[1], 128) * scales[:, :, None]
    turned = jnp.einsum("rbk,kj->rbj", blocks, hadamard_table(), precision=lax.Precision.HIGHEST)
    return turned.reshape(count, coded.shape[1]).astype(jnp.bfloat16)


def gelu_slope(value):
    cdf = 0.5 * (1.0 + jax.scipy.special.erf(value / math.sqrt(2.0)))
    pdf = jnp.exp(-0.5 * value * value) / math.sqrt(2.0 * math.pi)
    return cdf + value * pdf


def slope_grad(pre, grads):
    return (grads.astype(jnp.float32) * gelu_slope(pre)).astype(jnp.bfloat16)


def dot(a, b, dims):
    return lax.dot_general(a, b, (dims, ((), ())), preferred_element_type=jnp.float32)


def along_z(array, step, flip=False):
    pairs = [(2 * z + y, 2 * ((z + step) % 16) + (1 - y if flip else y)) for z in range(16) for y in range(2)]
    return lax.ppermute(array, TENSOR, pairs)


def swap_cores(array):
    return lax.ppermute(array, "c", SWAP)


def exchange(blocks):
    return lax.all_to_all(blocks, ("yh", "x"), 0, 0, tiled=True)


def copies(grad):
    return jnp.broadcast_to(grad[None], (8,) + grad.shape)


def places(pieces):
    z, core = lax.axis_index("z"), lax.axis_index("c")
    offsets = jnp.array([d for piece in pieces for d in piece], jnp.int32)
    block = lax.rem(z + offsets + 16, 16)
    return jnp.bitwise_xor(jnp.bitwise_and(block, 1), core) * 8 + block // 2


def gather_kernel(place_ref, a_ref, b_ref, c_ref, d_ref, e_ref, w_ref, rows_ref, far_ref):
    at = 0
    for piece in (a_ref, b_ref, c_ref, d_ref, e_ref):
        for i in range(piece.shape[0]):
            rows_ref[place_ref[at]] = piece[i]
            at += 1
    rows = rows_ref[8:16].reshape(256, 640)
    for j in range(0, 1152, 384):
        far_ref[:, j : j + 384] = jnp.dot(
            rows, w_ref[:, j : j + 384], preferred_element_type=jnp.float32
        ).astype(jnp.bfloat16)


def spread_kernel(place_ref, part_ref, *out_refs):
    at = 0
    for piece in out_refs:
        for i in range(piece.shape[0]):
            piece[i] = part_ref[place_ref[at]]
            at += 1


def gathered(own, w_in):
    a1, a0, a2, a3 = (along_z(own, step, flip=True) for step in (4, 0, -4, 8))
    stack = jnp.stack([a1, a0, a2, a3])
    pieces = (stack, along_z(stack, 1), along_z(stack, -1), along_z(stack[0:2], 2), along_z(stack[1:3], -2))
    return pl.pallas_call(
        gather_kernel,
        out_shape=(
            jax.ShapeDtypeStruct((16, 32, 640), jnp.bfloat16),
            jax.ShapeDtypeStruct((256, 1152), jnp.bfloat16),
        ),
        in_specs=[SMEM] + [VMEM] * 6,
        out_specs=(VMEM, VMEM),
        compiler_params=PARAMS,
        cost_estimate=pl.CostEstimate(flops=2 * 256 * 640 * 1152, bytes_accessed=4 * 1024 * 1024, transcendentals=0),
    )(places(PIECES), *pieces, w_in)


SENT = ((-4, 0, 4, 8), (-3, 1, 5, 9), (-5, -1, 3, 7), (2, 6), (-6, -2))


def scattered(part):
    shapes = [jax.ShapeDtypeStruct((len(s), 32, 640), jnp.bfloat16) for s in SENT]
    own, right, left, right2, left2 = pl.pallas_call(
        spread_kernel,
        out_shape=shapes,
        in_specs=[SMEM, VMEM],
        out_specs=[VMEM] * 5,
        compiler_params=PARAMS,
        cost_estimate=pl.CostEstimate(flops=0, bytes_accessed=1310720, transcendentals=0),
    )(places(SENT), part.reshape(16, 32, 640))
    right, left, right2, left2 = along_z(right, 1), along_z(left, -1), along_z(right2, 2), along_z(left2, -2)
    f = lambda v: v.astype(jnp.float32)
    near = f(own) + f(right) + f(left)
    low = (near[0] + f(left2[0])).astype(jnp.bfloat16)
    high = (near[2] + f(right2[1])).astype(jnp.bfloat16)
    apart = near[3].astype(jnp.bfloat16)
    low, high, apart = along_z(low, -4), along_z(high, 4), along_z(apart, 8)
    mine = near[1] + f(right2[0]) + f(left2[1])
    return mine + f(low) + f(high) + f(apart)


def shards(x_rotated, block_scales, grad_act, w_in):
    side = lax.axis_index("yl")
    grads = grad_act.reshape(2, 32, -1)
    grads_p = lax.dynamic_index_in_dim(grads, 1 - side, 0, keepdims=False)
    grads_o = lax.dynamic_index_in_dim(grads, side, 0, keepdims=False)
    own = decode(x_rotated, block_scales)
    rows_p, far_p = gathered(own, w_in)
    rows_p = rows_p.reshape(512, -1)
    rows_o = lax.ppermute(rows_p, "yl", SWAP)
    far_p = swap_cores(far_p)

    def near_sum(rows, far):
        near = dot(rows[:256], w_in, ((1,), (0,))) + far.astype(jnp.float32)
        return near.astype(jnp.bfloat16).reshape(8, 32, -1)

    def slopes(parts, grads):
        return slope_grad(jnp.sum(parts.astype(jnp.float32), axis=0), grads)

    parts_p = exchange(near_sum(rows_p, far_p))
    far_o = swap_cores(dot(rows_o[256:], w_in, ((1,), (0,))).astype(jnp.bfloat16))
    near_o = near_sum(rows_o, far_o)
    grad_p = slopes(parts_p, grads_p)
    mixed = exchange(jnp.concatenate([near_o, copies(grad_p)], axis=1))
    grad_o = slopes(mixed[:, :32], grads_o)
    mine_p = mixed[:, 32:].reshape(256, -1)
    mine_o = exchange(copies(grad_o)).reshape(256, -1)
    other_p = swap_cores(mine_p)
    pre_p = jnp.concatenate([mine_p, other_p])
    part_p = dot(pre_p, w_in, ((1,), (1,))).astype(jnp.bfloat16)
    part_p = lax.ppermute(part_p, "yl", SWAP)
    pre_o = jnp.concatenate([mine_o, swap_cores(mine_o)])
    part = (dot(pre_o, w_in, ((1,), (1,))) + part_p.astype(jnp.float32)).astype(jnp.bfloat16)
    grad_input = scattered(part)
    grad_weight = dot(rows_p, pre_p, ((0,), (0,))) + dot(rows_o, pre_o, ((0,), (0,)))
    return grad_input.astype(jnp.bfloat16), grad_weight.astype(jnp.bfloat16)


def solution(mesh):
    fine = Mesh(mesh.devices.reshape(SIZES), AXES)
    in_specs = (P(TENSOR, DP), P(TENSOR, DP), P(DP, TENSOR), P(DP, TENSOR))
    out_specs = (P(TENSOR, DP), P(DP, TENSOR))
    return jax.shard_map(shards, mesh=fine, in_specs=in_specs, out_specs=out_specs, check_vma=False)
```

```python
import math

import jax
import jax.numpy as jnp
from jax import lax
from jax.experimental import pallas as pl
from jax.experimental.pallas import tpu as pltpu
from jax.sharding import Mesh
from jax.sharding import PartitionSpec as P

AXES = ("yh", "x", "c", "z", "yl")
SIZES = (2, 4, 2, 16, 2)
DP = ("yh", "x", "c")
TENSOR = ("z", "yl")
SWAP = [(0, 1), (1, 0)]
PIECES = ((-4, 0, 4, 8), (-3, 1, 5, 9), (-5, -1, 3, 7), (2, 6), (-6, -2))
VMEM = pl.BlockSpec(memory_space=pltpu.VMEM)
SMEM = pl.BlockSpec(memory_space=pltpu.SMEM)
PARAMS = pltpu.CompilerParams(vmem_limit_bytes=24 * 1024 * 1024)


def hadamard_table():
    index = lax.iota(jnp.int32, 128)
    common = jnp.bitwise_and(index[:, None], index[None, :])
    parity = jnp.zeros((128, 128), jnp.int32)
    for shift in range(7):
        parity = parity + jnp.bitwise_and(jnp.right_shift(common, shift), 1)
    signs = 1.0 - 2.0 * (parity % 2).astype(jnp.float32)
    return signs / math.sqrt(128.0)


def decode(coded, scales):
    count = coded.shape[0]
    blocks = coded.astype(jnp.float32).reshape(count, scales.shape[1], 128) * scales[:, :, None]
    turned = jnp.einsum("rbk,kj->rbj", blocks, hadamard_table(), precision=lax.Precision.HIGHEST)
    return turned.reshape(count, coded.shape[1]).astype(jnp.bfloat16)


def gelu_slope(value):
    cdf = 0.5 * (1.0 + jax.scipy.special.erf(value / math.sqrt(2.0)))
    pdf = jnp.exp(-0.5 * value * value) / math.sqrt(2.0 * math.pi)
    return cdf + value * pdf


def slope_grad(pre, grads):
    return (grads.astype(jnp.float32) * gelu_slope(pre)).astype(jnp.bfloat16)


def dot(a, b, dims):
    return lax.dot_general(a, b, (dims, ((), ())), preferred_element_type=jnp.float32)


def along_z(array, step):
    return lax.ppermute(array, "z", [(z, (z + step) % 16) for z in range(16)])


def swap_cores(array):
    return lax.ppermute(array, "c", SWAP)


def exchange(blocks):
    return lax.all_to_all(blocks, ("yh", "x"), 0, 0, tiled=True)


def copies(grad):
    return jnp.broadcast_to(grad[None], (8,) + grad.shape)


def places(pieces):
    z, core = lax.axis_index("z"), lax.axis_index("c")
    offsets = jnp.array([d for piece in pieces for d in piece], jnp.int32)
    block = lax.rem(z + offsets + 16, 16)
    return jnp.bitwise_xor(jnp.bitwise_and(block, 1), core) * 8 + block // 2


def call(kernel, out_shape, count, flops, moved):
    return pl.pallas_call(
        kernel,
        out_shape=out_shape,
        in_specs=[SMEM] + [VMEM] * count,
        out_specs=[VMEM] * len(out_shape),
        compiler_params=PARAMS,
        cost_estimate=pl.CostEstimate(flops=flops, bytes_accessed=moved, transcendentals=0),
    )


def shape(*dims):
    return jax.ShapeDtypeStruct(dims, jnp.bfloat16)


def far_kernel(core_ref, rows_ref, w_ref, v_ref, far_ref):
    rows = rows_ref[:, 1 - core_ref[0]].reshape(256, 640)
    for i, weight in enumerate((w_ref, v_ref)):
        for j in range(0, 1152, 384):
            far_ref[:, 1152 * i + j : 1152 * i + j + 384] = jnp.dot(
                rows, weight[:, j : j + 384], preferred_element_type=jnp.float32
            ).astype(jnp.bfloat16)


def near_kernel(core_ref, rows_ref, w_ref, v_ref, far_ref, near_ref):
    rows = rows_ref[:, core_ref[0]].reshape(256, 640)
    for i, weight in enumerate((w_ref, v_ref)):
        for j in range(0, 1152, 384):
            at = slice(1152 * i + j, 1152 * i + j + 384)
            total = jnp.dot(rows, weight[:, j : j + 384], preferred_element_type=jnp.float32)
            near_ref[:, :, at] = (total + far_ref[:, at].astype(jnp.float32)).astype(jnp.bfloat16).reshape(8, 32, 384)


def input_part(pre_ref, w_ref, v_ref):
    nt = (((1,), (1,)), ((), ()))
    part = lax.dot_general(pre_ref[:, :1152], w_ref[...], nt, preferred_element_type=jnp.float32)
    part += lax.dot_general(pre_ref[:, 1152:], v_ref[...], nt, preferred_element_type=jnp.float32)
    return part.astype(jnp.bfloat16).reshape(8, 32, 640)


def part_kernel(core_ref, pre_ref, w_ref, v_ref, part_ref):
    part_ref[...] = input_part(pre_ref, w_ref, v_ref)


def spread_kernel(place_ref, mine_ref, pre_ref, w_ref, v_ref, *refs):
    part_ref = refs[-1]
    part_ref[:8] = mine_ref[...]
    part_ref[8:] = input_part(pre_ref, w_ref, v_ref)
    at = 0
    for piece in refs[:-1]:
        for i in range(piece.shape[0]):
            piece[i] = part_ref[place_ref[at]]
            at += 1


def spread(mine, pre, w_in, w_pair):
    shapes = [shape(len(piece), 32, 640) for piece in PIECES]
    return pl.pallas_call(
        spread_kernel,
        out_shape=shapes,
        in_specs=[SMEM] + [VMEM] * 4,
        out_specs=[VMEM] * 5,
        scratch_shapes=[pltpu.VMEM((16, 32, 640), jnp.bfloat16)],
        compiler_params=PARAMS,
        cost_estimate=pl.CostEstimate(flops=2 * 256 * 640 * 2304, bytes_accessed=6000000, transcendentals=0),
    )(places(PIECES), mine, pre, w_in, w_pair)


def summed_along_z(own, right, left, right2, left2):
    right, left, right2, left2 = along_z(right, 1), along_z(left, -1), along_z(right2, 2), along_z(left2, -2)
    f = lambda v: v.astype(jnp.float32)
    near = f(own) + f(right) + f(left)
    low = (near[0] + f(left2[0])).astype(jnp.bfloat16)
    high = (near[2] + f(right2[1])).astype(jnp.bfloat16)
    apart = near[3].astype(jnp.bfloat16)
    low, high, apart = along_z(low, -4), along_z(high, 4), along_z(apart, 8)
    mine = near[1] + f(right2[0]) + f(left2[1])
    return (mine + f(low) + f(high) + f(apart)).astype(jnp.bfloat16)


def swap_pair(array):
    return lax.ppermute(array, "yl", SWAP)


def shards(x_rotated, block_scales, grad_act, w_in):
    side, core = lax.axis_index("yl"), lax.axis_index("c")
    w_pair = swap_pair(w_in)
    own = decode(x_rotated, block_scales)
    rows = lax.all_gather(own, "z", axis=0, tiled=True).reshape(8, 2, 32, 640)
    at = jnp.reshape(core, (1,)).astype(jnp.int32)
    flops = 2 * 256 * 640 * 2304
    (far,) = call(far_kernel, [shape(256, 2304)], 3, flops, 6000000)(at, rows, w_in, w_pair)
    far = swap_cores(far)
    (near,) = call(near_kernel, [shape(8, 32, 2304)], 4, flops, 6000000)(at, rows, w_in, w_pair, far)
    parts = exchange(near)
    grads = grad_act.reshape(2, 32, 1152)
    lent = lax.dynamic_index_in_dim(grads, 1 - side, 0, keepdims=False)
    kept = lax.dynamic_index_in_dim(grads, side, 0, keepdims=False)
    grads = jnp.concatenate([kept, swap_pair(lent)], axis=1)
    pre = jnp.sum(parts.astype(jnp.float32), axis=0)
    mine = exchange(copies(slope_grad(pre, grads))).reshape(256, 2304)
    other = swap_cores(mine)
    (part,) = call(part_kernel, [shape(8, 32, 640)], 3, flops, 6000000)(at, mine, w_in, w_pair)
    pieces = spread(part, other, w_in, w_pair)
    rows_mine = lax.dynamic_index_in_dim(rows, core, 1, keepdims=False).reshape(256, 640)
    rows_other = lax.dynamic_index_in_dim(rows, 1 - core, 1, keepdims=False).reshape(256, 640)
    tn = ((0,), (0,))
    lent = dot(rows_mine, mine[:, 1152:], tn) + dot(rows_other, other[:, 1152:], tn)
    lent = swap_pair(lent.astype(jnp.bfloat16))
    kept = dot(rows_mine, mine[:, :1152], tn) + dot(rows_other, other[:, :1152], tn)
    grad_weight = (kept + lent.astype(jnp.float32)).astype(jnp.bfloat16)
    return summed_along_z(*pieces), grad_weight


def solution(mesh):
    fine = Mesh(mesh.devices.reshape(SIZES), AXES)
    in_specs = (P(TENSOR, DP), P(TENSOR, DP), P(DP, TENSOR), P(DP, TENSOR))
    out_specs = (P(TENSOR, DP), P(DP, TENSOR))
    return jax.shard_map(shards, mesh=fine, in_specs=in_specs, out_specs=out_specs, check_vma=False)
```

```python
import math

import jax
import jax.numpy as jnp
from jax import lax
from jax.experimental import pallas as pl
from jax.experimental.pallas import tpu as pltpu
from jax.sharding import Mesh
from jax.sharding import PartitionSpec as P

AXES = ("yh", "x", "c", "za", "zl", "yl")
SIZES = (2, 4, 2, 4, 4, 2)
DP = ("yh", "x", "c")
TENSOR = ("za", "zl", "yl")
SWAP = [(0, 1), (1, 0)]
VMEM = pl.BlockSpec(memory_space=pltpu.VMEM)
SMEM = pl.BlockSpec(memory_space=pltpu.SMEM)
ANY = pl.BlockSpec(memory_space=pl.ANY)
PARAMS = pltpu.CompilerParams(vmem_limit_bytes=16 * 1024 * 1024)


def hadamard_table():
    index = lax.iota(jnp.int32, 128)
    common = jnp.bitwise_and(index[:, None], index[None, :])
    parity = jnp.zeros((128, 128), jnp.int32)
    for shift in range(7):
        parity = parity + jnp.bitwise_and(jnp.right_shift(common, shift), 1)
    signs = 1.0 - 2.0 * (parity % 2).astype(jnp.float32)
    return signs / math.sqrt(128.0)


def decode(coded, scales):
    count = coded.shape[0]
    blocks = coded.astype(jnp.float32).reshape(count, scales.shape[1], 128) * scales[:, :, None]
    turned = jnp.einsum("rbk,kj->rbj", blocks, hadamard_table(), precision=lax.Precision.HIGHEST)
    return turned.reshape(count, coded.shape[1]).astype(jnp.bfloat16)


def gelu_slope(value):
    cdf = 0.5 * (1.0 + jax.scipy.special.erf(value / math.sqrt(2.0)))
    pdf = jnp.exp(-0.5 * value * value) / math.sqrt(2.0 * math.pi)
    return cdf + value * pdf


def slope_grad(pre, grads):
    return (grads.astype(jnp.float32) * gelu_slope(pre)).astype(jnp.bfloat16)


def dot(a, b, dims):
    return lax.dot_general(a, b, (dims, ((), ())), preferred_element_type=jnp.float32)


def along_z(array, step):
    return lax.ppermute(array, ("za", "zl"), [(z, (z + step) % 16) for z in range(16)])


def swap_cores(array):
    return lax.ppermute(array, "c", SWAP)


def exchange(blocks):
    return lax.all_to_all(blocks, ("yh", "x"), 0, 0, tiled=True)


def copies(grad):
    return jnp.broadcast_to(grad[None], (8,) + grad.shape)


def call(kernel, out_shape, count, flops, moved, after=0):
    return pl.pallas_call(
        kernel,
        out_shape=out_shape,
        in_specs=[SMEM] + [VMEM] * count + [ANY] * after,
        out_specs=[VMEM] * len(out_shape),
        compiler_params=PARAMS,
        cost_estimate=pl.CostEstimate(flops=flops, bytes_accessed=moved, transcendentals=0),
    )


def shape(*dims):
    return jax.ShapeDtypeStruct(dims, jnp.bfloat16)


def far_kernel(core_ref, rows_ref, w_ref, v_ref, far_ref):
    rows = rows_ref[:, 1 - core_ref[0]].reshape(256, 640)
    for i, weight in enumerate((w_ref, v_ref)):
        for j in range(0, 1152, 384):
            far_ref[:, 1152 * i + j : 1152 * i + j + 384] = jnp.dot(
                rows, weight[:, j : j + 384], preferred_element_type=jnp.float32
            ).astype(jnp.bfloat16)


def near_kernel(core_ref, rows_ref, w_ref, v_ref, near_ref):
    rows = rows_ref[:, core_ref[0]].reshape(256, 640)
    for i, weight in enumerate((w_ref, v_ref)):
        for j in range(0, 1152, 384):
            near_ref[:, 1152 * i + j : 1152 * i + j + 384] = jnp.dot(
                rows, weight[:, j : j + 384], preferred_element_type=jnp.float32
            ).astype(jnp.bfloat16)


def input_part(pre_ref, w_ref, v_ref):
    nt = (((1,), (1,)), ((), ()))
    part = lax.dot_general(pre_ref[:, :1152], w_ref[...], nt, preferred_element_type=jnp.float32)
    part += lax.dot_general(pre_ref[:, 1152:], v_ref[...], nt, preferred_element_type=jnp.float32)
    return part.astype(jnp.bfloat16).reshape(8, 32, 640)


def part_kernel(core_ref, pre_ref, w_ref, v_ref, part_ref):
    part_ref[...] = input_part(pre_ref, w_ref, v_ref)


def weight_terms(core, rows_ref, mine_ref, other_ref, first):
    tn = (((0,), (0,)), ((), ()))
    left = [rows_ref[:, at].reshape(256, 640) for at in (core, 1 - core)]
    for j in range(0, 1152, 384):
        at = slice(first + j, first + j + 384)
        total = lax.dot_general(left[0], mine_ref[:, at], tn, preferred_element_type=jnp.float32)
        yield slice(j, j + 384), total + lax.dot_general(left[1], other_ref[:, at], tn, preferred_element_type=jnp.float32)


def spread_kernel(place_ref, rows_ref, part_ref, mine_ref, pre_ref, w_ref, v_ref, lent_ref, own_ref, right2_ref, left2_ref, right_ref, left_ref, all_ref):
    core, place = place_ref[0], place_ref[1]
    for at, total in weight_terms(core, rows_ref, mine_ref, pre_ref, 1152):
        lent_ref[:, at] = total.astype(jnp.bfloat16)
    other = input_part(pre_ref, w_ref, v_ref)
    for low in range(2):
        for high in range(4):
            all_ref[2 * low + core, high] = part_ref[2 * high + low]
            all_ref[2 * low + 1 - core, high] = other[2 * high + low]
    own_ref[...] = all_ref[place]
    right_ref[...] = all_ref[lax.rem(place + 1, 4)]
    left_ref[...] = all_ref[lax.rem(place + 3, 4)]
    apart = lax.rem(place + 2, 4)
    right2_ref[...] = all_ref[apart, 0:2]
    left2_ref[...] = all_ref[apart, 2:4]


def spread(place, rows, part, mine, pre, w_in, w_pair):
    return pl.pallas_call(
        spread_kernel,
        out_shape=[shape(640, 1152)] + [shape(count, 32, 640) for count in (4, 2, 2, 4, 4)],
        in_specs=[SMEM] + [VMEM] * 6,
        out_specs=[VMEM] * 6,
        scratch_shapes=[pltpu.VMEM((4, 4, 32, 640), jnp.bfloat16)],
        compiler_params=PARAMS,
        cost_estimate=pl.CostEstimate(flops=4 * 256 * 640 * 2304, bytes_accessed=9000000, transcendentals=0),
    )(place, rows, part, mine, pre, w_in, w_pair)


def kept_kernel(core_ref, rows_ref, mine_ref, other_ref, out_ref):
    for at, total in weight_terms(core_ref[0], rows_ref, mine_ref, other_ref, 0):
        out_ref[:, at] = total.astype(jnp.bfloat16)


def summed_near(own, right2, left2, right, left):
    right2, left2, right, left = along_z(right2, 2), along_z(left2, -2), along_z(right, 1), along_z(left, -1)
    f = lambda v: v.astype(jnp.float32)
    return (f(own) + f(right) + f(left) + f(jnp.concatenate([right2, left2]))).astype(jnp.bfloat16)


def swap_pair(array):
    return lax.ppermute(array, "yl", SWAP)


def shards(x_rotated, block_scales, grad_act, w_in):
    side, core = lax.axis_index("yl"), lax.axis_index("c")
    w_pair = swap_pair(w_in)
    own = decode(x_rotated, block_scales)
    rows = lax.all_gather(own, ("za", "zl"), axis=0, tiled=True).reshape(8, 2, 32, 640)
    at = jnp.reshape(core, (1,)).astype(jnp.int32)
    flops = 2 * 256 * 640 * 2304
    (far,) = call(far_kernel, [shape(256, 2304)], 3, flops, 6000000)(at, rows, w_in, w_pair)
    grads = grad_act.reshape(2, 32, 1152)
    lent = lax.dynamic_index_in_dim(grads, 1 - side, 0, keepdims=False)
    kept = lax.dynamic_index_in_dim(grads, side, 0, keepdims=False)
    far, lent = swap_cores(far), swap_pair(lent)
    grads = jnp.concatenate([kept, lent], axis=1)
    (near,) = call(near_kernel, [shape(256, 2304)], 3, flops, 6000000)(at, rows, w_in, w_pair)
    near = (near.astype(jnp.float32) + far.astype(jnp.float32)).astype(jnp.bfloat16).reshape(8, 32, 2304)
    pre = jnp.sum(exchange(near).astype(jnp.float32), axis=0)
    mine = exchange(copies(slope_grad(pre, grads))).reshape(256, 2304)
    other = swap_cores(mine)
    (part,) = call(part_kernel, [shape(8, 32, 640)], 3, flops, 6000000)(at, mine, w_in, w_pair)
    place = jnp.stack([core, lax.axis_index("zl")]).astype(jnp.int32)
    lent, *pieces = spread(place, rows, part, mine, other, w_in, w_pair)
    lent = swap_pair(lent)
    near = summed_near(*pieces)
    blocks = lax.all_to_all(near, "za", 0, 0, tiled=True)
    (kept,) = call(kept_kernel, [shape(640, 1152)], 3, flops, 4000000)(at, rows, mine, other)
    grad_weight = (kept.astype(jnp.float32) + lent.astype(jnp.float32)).astype(jnp.bfloat16)
    blocks, grad_weight = lax.optimization_barrier((blocks, grad_weight))
    return jnp.sum(blocks.astype(jnp.float32), axis=0).astype(jnp.bfloat16), grad_weight


def solution(mesh):
    fine = Mesh(mesh.devices.reshape(SIZES), AXES)
    in_specs = (P(TENSOR, DP), P(TENSOR, DP), P(DP, TENSOR), P(DP, TENSOR))
    out_specs = (P(TENSOR, DP), P(DP, TENSOR))
    return jax.shard_map(shards, mesh=fine, in_specs=in_specs, out_specs=out_specs, check_vma=False)
```

```python
import math

import jax
import jax.numpy as jnp
from jax import lax
from jax.experimental import pallas as pl
from jax.experimental.pallas import tpu as pltpu
from jax.sharding import Mesh
from jax.sharding import PartitionSpec as P

AXES = ("yh", "x", "c", "za", "zl", "yl")
SIZES = (2, 4, 2, 4, 4, 2)
DP = ("yh", "x", "c")
TENSOR = ("za", "zl", "yl")
SWAP = [(0, 1), (1, 0)]
VMEM = pl.BlockSpec(memory_space=pltpu.VMEM)
SMEM = pl.BlockSpec(memory_space=pltpu.SMEM)
ANY = pl.BlockSpec(memory_space=pl.ANY)
PARAMS = pltpu.CompilerParams(vmem_limit_bytes=16 * 1024 * 1024)


def hadamard_table():
    index = lax.iota(jnp.int32, 128)
    common = jnp.bitwise_and(index[:, None], index[None, :])
    parity = jnp.zeros((128, 128), jnp.int32)
    for shift in range(7):
        parity = parity + jnp.bitwise_and(jnp.right_shift(common, shift), 1)
    signs = 1.0 - 2.0 * (parity % 2).astype(jnp.float32)
    return signs / math.sqrt(128.0)


def decode(coded, scales):
    count = coded.shape[0]
    blocks = coded.astype(jnp.float32).reshape(count, scales.shape[1], 128) * scales[:, :, None]
    turned = jnp.einsum("rbk,kj->rbj", blocks, hadamard_table(), precision=lax.Precision.HIGHEST)
    return turned.reshape(count, coded.shape[1]).astype(jnp.bfloat16)


def gelu_slope(value):
    cdf = 0.5 * (1.0 + jax.scipy.special.erf(value / math.sqrt(2.0)))
    pdf = jnp.exp(-0.5 * value * value) / math.sqrt(2.0 * math.pi)
    return cdf + value * pdf


def slope_grad(pre, grads):
    return (grads.astype(jnp.float32) * gelu_slope(pre)).astype(jnp.bfloat16)


def dot(a, b, dims):
    return lax.dot_general(a, b, (dims, ((), ())), preferred_element_type=jnp.float32)


def z_and_core(array, target):
    pairs = [(16 * core + z, 16 * core + target(z, core) % 16) for core in range(2) for z in range(16)]
    return lax.ppermute(array, ("c", "za", "zl"), pairs)


def swap_cores(array):
    return lax.ppermute(array, "c", SWAP)


def exchange(blocks):
    return lax.all_to_all(blocks, ("yh", "x"), 0, 0, tiled=True)


def copies(grad):
    return jnp.broadcast_to(grad[None], (8,) + grad.shape)


def call(kernel, out_shape, count, flops, moved, after=0):
    return pl.pallas_call(
        kernel,
        out_shape=out_shape,
        in_specs=[SMEM] + [VMEM] * count + [ANY] * after,
        out_specs=[VMEM] * len(out_shape),
        compiler_params=PARAMS,
        cost_estimate=pl.CostEstimate(flops=flops, bytes_accessed=moved, transcendentals=0),
    )


def shape(*dims):
    return jax.ShapeDtypeStruct(dims, jnp.bfloat16)


def far_kernel(core_ref, rows_ref, w_ref, v_ref, far_ref):
    rows = rows_ref[:, 1 - core_ref[0]].reshape(256, 640)
    for i, weight in enumerate((w_ref, v_ref)):
        for j in range(0, 1152, 384):
            far_ref[:, 1152 * i + j : 1152 * i + j + 384] = jnp.dot(
                rows, weight[:, j : j + 384], preferred_element_type=jnp.float32
            ).astype(jnp.bfloat16)


def near_kernel(core_ref, rows_ref, w_ref, v_ref, near_ref):
    rows = rows_ref[:, core_ref[0]].reshape(256, 640)
    for i, weight in enumerate((w_ref, v_ref)):
        for j in range(0, 1152, 384):
            near_ref[:, 1152 * i + j : 1152 * i + j + 384] = jnp.dot(
                rows, weight[:, j : j + 384], preferred_element_type=jnp.float32
            ).astype(jnp.bfloat16)


def input_part(pre_ref, w_ref, v_ref):
    nt = (((1,), (1,)), ((), ()))
    part = lax.dot_general(pre_ref[:, :1152], w_ref[...], nt, preferred_element_type=jnp.float32)
    part += lax.dot_general(pre_ref[:, 1152:], v_ref[...], nt, preferred_element_type=jnp.float32)
    return part.astype(jnp.bfloat16).reshape(8, 32, 640)


def part_kernel(class_ref, pre_ref, w_ref, v_ref, w2_ref, v2_ref, first_ref, second_ref, kept_ref, lent_ref):
    for i, weights in enumerate(((w_ref, v_ref), (w2_ref, v2_ref))):
        part = input_part(pre_ref, *weights).reshape(4, 2, 32, 640)
        for out_ref, which in ((first_ref, class_ref[0]), (second_ref, class_ref[1])):

            @pl.when(which == 0)
            def _():
                out_ref[i] = part[:, 0]

            @pl.when(which == 1)
            def _():
                out_ref[i] = part[:, 1]

    kept_ref[...] = pre_ref[:, :1152]
    lent_ref[...] = pre_ref[:, 1152:]


def weight_terms(terms):
    tn = (((0,), (0,)), ((), ()))
    for j in range(0, 1152, 384):
        at = slice(j, j + 384)
        yield at, sum(lax.dot_general(rows, grad[:, at], tn, preferred_element_type=jnp.float32) for rows, grad in terms)


def kept_kernel(at_ref, rows_ref, mine_ref, other_ref, out_ref):
    left = [rows_ref[:, at].reshape(256, 640) for at in (at_ref[0], 1 - at_ref[0])]
    for at, total in weight_terms(list(zip(left, (mine_ref, other_ref)))):
        out_ref[:, at] = total.astype(jnp.bfloat16)


def weight_kernel(at_ref, rows_ref, mine_ref, other_ref, other2_ref, kept_ref, out_ref):
    last = rows_ref[:, 1 - at_ref[0]].reshape(2, 128, 640)
    left = [rows_ref[:, at_ref[0]].reshape(256, 640), last[0], last[1]]
    for at, total in weight_terms(list(zip(left, (mine_ref, other_ref, other2_ref)))):
        out_ref[:, at] = (total + kept_ref[:, at].astype(jnp.float32)).astype(jnp.bfloat16)


def swap_pair(array):
    return lax.ppermute(array, "yl", SWAP)


def shards(x_rotated, block_scales, grad_act, w_in):
    side, core, zl = lax.axis_index("yl"), lax.axis_index("c"), lax.axis_index("zl")
    at = jnp.reshape(jnp.bitwise_and(core + zl, 1), (1,)).astype(jnp.int32)
    w_pair = swap_pair(w_in)
    own = decode(x_rotated, block_scales)
    rows = lax.all_gather(own, ("za", "zl"), axis=0, tiled=True).reshape(8, 2, 32, 640)
    flops = 2 * 256 * 640 * 2304
    (far,) = call(far_kernel, [shape(256, 2304)], 3, flops, 6000000)(at, rows, w_in, w_pair)
    pairs = [(4 * c + z, 4 * ((c + z) % 2) + z) for c in range(2) for z in range(4)]
    grads = lax.ppermute(grad_act, ("c", "zl"), pairs).reshape(2, 32, 1152)
    lent = lax.dynamic_index_in_dim(grads, 1 - side, 0, keepdims=False)
    kept = lax.dynamic_index_in_dim(grads, side, 0, keepdims=False)
    far, lent = swap_cores(far), swap_pair(lent)
    grads = jnp.concatenate([kept, lent], axis=1)
    (near,) = call(near_kernel, [shape(256, 2304)], 3, flops, 6000000)(at, rows, w_in, w_pair)
    near = (near.astype(jnp.float32) + far.astype(jnp.float32)).astype(jnp.bfloat16).reshape(8, 32, 2304)
    w_core, w_pair_core = swap_cores(w_in), swap_cores(w_pair)
    pre = jnp.sum(exchange(near).astype(jnp.float32), axis=0)
    mine = exchange(copies(slope_grad(pre, grads))).reshape(256, 2304)

    classes = jnp.stack([jnp.bitwise_and(zl + 2 - core, 3), jnp.bitwise_and(zl + 3 * core, 3)])
    classes = jnp.right_shift(classes, 1).astype(jnp.int32)
    shapes = [shape(2, 4, 32, 640), shape(2, 4, 32, 640), shape(256, 1152), shape(256, 1152)]
    first, second, mine, lent = call(part_kernel, shapes, 5, 2 * flops, 9000000)(
        classes, mine, w_in, w_pair, w_core, w_pair_core
    )
    first = z_and_core(first, lambda z, c: z + 1 if c else z + (2 if z % 2 == 0 else -2))
    second = z_and_core(second, lambda z, c: z - c)
    mine_pair = swap_pair(lent)
    rows_pair, _ = lax.optimization_barrier((rows, lent))
    rows_pair = swap_pair(rows_pair)
    near = first.astype(jnp.float32) + second.astype(jnp.float32)
    lent, other = lax.optimization_barrier((near[1].astype(jnp.bfloat16), swap_cores(mine)))
    near = (near[0] + swap_cores(lent).astype(jnp.float32)).astype(jnp.bfloat16)
    blocks = lax.all_to_all(near, "za", 0, 0, tiled=True)
    other_pair = [swap_cores(mine_pair.reshape(2, 128, 1152)[i // 576]) for i in (0, 576)]
    (kept,) = call(kept_kernel, [shape(640, 1152)], 3, flops, 5000000)(at, rows, mine, other)
    (grad_weight,) = call(weight_kernel, [shape(640, 1152)], 5, flops, 5000000)(at, rows_pair, mine_pair, *other_pair, kept)
    blocks, grad_weight = lax.optimization_barrier((blocks, grad_weight))
    return jnp.sum(blocks.astype(jnp.float32), axis=0).astype(jnp.bfloat16), grad_weight


def solution(mesh):
    fine = Mesh(mesh.devices.reshape(SIZES), AXES)
    in_specs = (P(TENSOR, DP), P(TENSOR, DP), P(DP, TENSOR), P(DP, TENSOR))
    out_specs = (P(TENSOR, DP), P(DP, TENSOR))
    return jax.shard_map(shards, mesh=fine, in_specs=in_specs, out_specs=out_specs, check_vma=False)
```

```python
import math

import jax
import jax.numpy as jnp
from jax import lax
from jax.experimental import pallas as pl
from jax.experimental.pallas import tpu as pltpu
from jax.sharding import Mesh
from jax.sharding import PartitionSpec as P

AXES = ("yh", "x", "c", "za", "zl", "yl")
SIZES = (2, 4, 2, 4, 4, 2)
DP = ("yh", "x", "c")
TENSOR = ("za", "zl", "yl")
SWAP = [(0, 1), (1, 0)]
VMEM = pl.BlockSpec(memory_space=pltpu.VMEM)
SMEM = pl.BlockSpec(memory_space=pltpu.SMEM)
ANY = pl.BlockSpec(memory_space=pl.ANY)
PARAMS = pltpu.CompilerParams(vmem_limit_bytes=16 * 1024 * 1024)


def hadamard_table():
    index = lax.iota(jnp.int32, 128)
    common = jnp.bitwise_and(index[:, None], index[None, :])
    parity = jnp.zeros((128, 128), jnp.int32)
    for shift in range(7):
        parity = parity + jnp.bitwise_and(jnp.right_shift(common, shift), 1)
    signs = 1.0 - 2.0 * (parity % 2).astype(jnp.float32)
    return signs / math.sqrt(128.0)


def decode(coded, scales):
    count = coded.shape[0]
    blocks = coded.astype(jnp.float32).reshape(count, scales.shape[1], 128) * scales[:, :, None]
    turned = jnp.einsum("rbk,kj->rbj", blocks, hadamard_table(), precision=lax.Precision.HIGHEST)
    return turned.reshape(count, coded.shape[1]).astype(jnp.bfloat16)


def gelu_slope(value):
    cdf = 0.5 * (1.0 + jax.scipy.special.erf(value / math.sqrt(2.0)))
    pdf = jnp.exp(-0.5 * value * value) / math.sqrt(2.0 * math.pi)
    return cdf + value * pdf


def slope_grad(pre, grads):
    return (grads.astype(jnp.float32) * gelu_slope(pre)).astype(jnp.bfloat16)


def dot(a, b, dims):
    return lax.dot_general(a, b, (dims, ((), ())), preferred_element_type=jnp.float32)


def z_and_core(array, target):
    pairs = [(16 * core + z, 16 * core + target(z, core) % 16) for core in range(2) for z in range(16)]
    return lax.ppermute(array, ("c", "za", "zl"), pairs)


def swap_cores(array):
    return lax.ppermute(array, "c", SWAP)


def exchange(blocks):
    return lax.all_to_all(blocks, ("yh", "x"), 0, 0, tiled=True)


def copies(grad):
    return jnp.broadcast_to(grad[None], (8,) + grad.shape)


def call(kernel, out_shape, count, flops, moved, after=0):
    return pl.pallas_call(
        kernel,
        out_shape=out_shape,
        in_specs=[SMEM] + [VMEM] * count + [ANY] * after,
        out_specs=[VMEM] * len(out_shape),
        compiler_params=PARAMS,
        cost_estimate=pl.CostEstimate(flops=flops, bytes_accessed=moved, transcendentals=0),
    )


def shape(*dims):
    return jax.ShapeDtypeStruct(dims, jnp.bfloat16)


def far_kernel(core_ref, rows_ref, w_ref, v_ref, far_ref):
    rows = rows_ref[:, 1 - core_ref[0]].reshape(256, 640)
    for i, weight in enumerate((w_ref, v_ref)):
        for j in range(0, 1152, 384):
            far_ref[:, 1152 * i + j : 1152 * i + j + 384] = jnp.dot(
                rows, weight[:, j : j + 384], preferred_element_type=jnp.float32
            ).astype(jnp.bfloat16)


def near_kernel(core_ref, rows_ref, w_ref, v_ref, near_ref):
    rows = rows_ref[:, core_ref[0]].reshape(256, 640)
    for i, weight in enumerate((w_ref, v_ref)):
        for j in range(0, 1152, 384):
            near_ref[:, 1152 * i + j : 1152 * i + j + 384] = jnp.dot(
                rows, weight[:, j : j + 384], preferred_element_type=jnp.float32
            ).astype(jnp.bfloat16)


def input_part(pre_ref, w_ref, v_ref):
    nt = (((1,), (1,)), ((), ()))
    part = lax.dot_general(pre_ref[:, :1152], w_ref[...], nt, preferred_element_type=jnp.float32)
    part += lax.dot_general(pre_ref[:, 1152:], v_ref[...], nt, preferred_element_type=jnp.float32)
    return part.astype(jnp.bfloat16).reshape(8, 32, 640)


def part_kernel(class_ref, w_ref, v_ref, pre_hbm, w2_hbm, v2_hbm, first_ref, second_ref, kept_ref, lent_ref, pre_ref, w2_ref, v2_ref, part_ref, sems):
    fetches = []
    for i, (far, here) in enumerate(((pre_hbm, pre_ref), (w2_hbm, w2_ref), (v2_hbm, v2_ref))):
        rows = here.shape[0] // 4
        for j in range(4):
            at = pl.ds(rows * j, rows)
            fetches.append(pltpu.make_async_copy(far.at[at], here.at[at], sems.at[4 * i + j]))
            fetches[-1].start()
    for fetch in fetches[:4]:
        fetch.wait()
    kept_ref[...] = pre_ref[:, :1152]
    lent_ref[...] = pre_ref[:, 1152:]
    for i in range(2):
        if i == 1:
            for fetch in fetches[4:]:
                fetch.wait()
        part_ref[...] = input_part(pre_ref, *((w_ref, v_ref), (w2_ref, v2_ref))[i]).reshape(4, 2, 32, 640)
        first_ref[i] = part_ref[:, class_ref[0]]
        second_ref[i] = part_ref[:, class_ref[1]]


def parts_of(classes, mine, w_in, w_pair, w_core, w_pair_core):
    return pl.pallas_call(
        part_kernel,
        out_shape=[shape(2, 4, 32, 640), shape(2, 4, 32, 640), shape(256, 1152), shape(256, 1152)],
        in_specs=[SMEM] + [VMEM] * 2 + [ANY] * 3,
        out_specs=[VMEM] * 4,
        scratch_shapes=[pltpu.VMEM((256, 2304), jnp.bfloat16)]
        + [pltpu.VMEM((640, 1152), jnp.bfloat16)] * 2
        + [pltpu.VMEM((4, 2, 32, 640), jnp.bfloat16), pltpu.SemaphoreType.DMA((12,))],
        compiler_params=PARAMS,
        cost_estimate=pl.CostEstimate(flops=4 * 256 * 640 * 2304, bytes_accessed=9000000, transcendentals=0),
    )(classes, w_in, w_pair, mine, w_core, w_pair_core)


def weight_terms(terms):
    tn = (((0,), (0,)), ((), ()))
    for j in range(0, 1152, 384):
        at = slice(j, j + 384)
        yield at, sum(lax.dot_general(rows, grad[:, at], tn, preferred_element_type=jnp.float32) for rows, grad in terms)


def kept_kernel(at_ref, rows_ref, mine_ref, other_ref, out_ref):
    left = [rows_ref[:, at].reshape(256, 640) for at in (at_ref[0], 1 - at_ref[0])]
    for at, total in weight_terms(list(zip(left, (mine_ref, other_ref)))):
        out_ref[:, at] = total.astype(jnp.bfloat16)


def weight_kernel(at_ref, rows_ref, mine_ref, other_ref, other2_ref, kept_ref, out_ref):
    last = rows_ref[:, 1 - at_ref[0]].reshape(2, 128, 640)
    left = [rows_ref[:, at_ref[0]].reshape(256, 640), last[0], last[1]]
    for at, total in weight_terms(list(zip(left, (mine_ref, other_ref, other2_ref)))):
        out_ref[:, at] = (total + kept_ref[:, at].astype(jnp.float32)).astype(jnp.bfloat16)


def swap_pair(array):
    return lax.ppermute(array, "yl", SWAP)


def shards(x_rotated, block_scales, grad_act, w_in):
    side, core, zl = lax.axis_index("yl"), lax.axis_index("c"), lax.axis_index("zl")
    at = jnp.reshape(jnp.bitwise_and(core + zl, 1), (1,)).astype(jnp.int32)
    w_pair = swap_pair(w_in)
    own = decode(x_rotated, block_scales)
    rows = lax.all_gather(own, ("za", "zl"), axis=0, tiled=True).reshape(8, 2, 32, 640)
    flops = 2 * 256 * 640 * 2304
    (far,) = call(far_kernel, [shape(256, 2304)], 3, flops, 6000000)(at, rows, w_in, w_pair)
    pairs = [(4 * c + z, 4 * ((c + z) % 2) + z) for c in range(2) for z in range(4)]
    grads = lax.ppermute(grad_act, ("c", "zl"), pairs).reshape(2, 32, 1152)
    lent = lax.dynamic_index_in_dim(grads, 1 - side, 0, keepdims=False)
    kept = lax.dynamic_index_in_dim(grads, side, 0, keepdims=False)
    far, lent = swap_cores(far), swap_pair(lent)
    grads = jnp.concatenate([kept, lent], axis=1)
    (near,) = call(near_kernel, [shape(256, 2304)], 3, flops, 6000000)(at, rows, w_in, w_pair)
    near = (near.astype(jnp.float32) + far.astype(jnp.float32)).astype(jnp.bfloat16).reshape(8, 32, 2304)
    w_core, w_pair_core = swap_cores(w_in), swap_cores(w_pair)
    pre = jnp.sum(exchange(near).astype(jnp.float32), axis=0)
    mine = exchange(copies(slope_grad(pre, grads))).reshape(256, 2304)

    classes = jnp.stack([jnp.bitwise_and(zl + 2 - core, 3), jnp.bitwise_and(zl + 3 * core, 3)])
    classes = jnp.right_shift(classes, 1).astype(jnp.int32)
    first, second, mine, lent = parts_of(classes, mine, w_in, w_pair, w_core, w_pair_core)
    first = z_and_core(first, lambda z, c: z + 1 if c else z + (2 if z % 2 == 0 else -2))
    second = z_and_core(second, lambda z, c: z - c)
    mine_pair = swap_pair(lent)
    rows_pair, _ = lax.optimization_barrier((rows, lent))
    rows_pair = swap_pair(rows_pair)
    near = first.astype(jnp.float32) + second.astype(jnp.float32)
    lent, other = lax.optimization_barrier((near[1].astype(jnp.bfloat16), swap_cores(mine)))
    near = (near[0] + swap_cores(lent).astype(jnp.float32)).astype(jnp.bfloat16)
    blocks = lax.all_to_all(near, "za", 0, 0, tiled=True)
    other_pair = [swap_cores(mine_pair.reshape(2, 128, 1152)[i // 576]) for i in (0, 576)]
    (kept,) = call(kept_kernel, [shape(640, 1152)], 3, flops, 5000000)(at, rows, mine, other)
    (grad_weight,) = call(weight_kernel, [shape(640, 1152)], 5, flops, 5000000)(at, rows_pair, mine_pair, *other_pair, kept)
    blocks, grad_weight = lax.optimization_barrier((blocks, grad_weight))
    return jnp.sum(blocks.astype(jnp.float32), axis=0).astype(jnp.bfloat16), grad_weight


def solution(mesh):
    fine = Mesh(mesh.devices.reshape(SIZES), AXES)
    in_specs = (P(TENSOR, DP), P(TENSOR, DP), P(DP, TENSOR), P(DP, TENSOR))
    out_specs = (P(TENSOR, DP), P(DP, TENSOR))
    return jax.shard_map(shards, mesh=fine, in_specs=in_specs, out_specs=out_specs, check_vma=False)
```
